32 devices in a mesh: slab: 8 (over y, x, core), grp: 4 (over z).
Axes of the slice: x: 2, y: 2, z: 4, core: 2. Of those that a mesh axis runs over, the one named last changes fastest.
Arguments:
- images: float32 [32, 512, 512], P(('slab', 'grp')), may hold values from -6 to 6
- crossing_row: int32 [32, 1024], P(('slab', 'grp')), may hold values from 0 to 511
- crossing_dest: int32 [32, 1024, 1], P(('slab', 'grp')), may hold values from 0 to 31; in each aligned block of 1024 rows (0 to 1023, 1024 to 2047, ..., all dimensions but the last counted through in order) at most 64 rows name the same one
- crossing_line: int32 [32, 1024], P(('slab', 'grp')), may hold values from 0 to 127
- interp_weight: bfloat16 [32, 1024, 64], P(('slab', 'grp')), may hold values from 0 to 1
Outputs:
- reconstruction: float32 [2, 512, 512, 512], P(None, 'slab', 'grp')
The draws below stay inside these ranges and needn't reach their ends.
Inputs may be any that keep to these rules, and one draw needn't show every extreme that they name: `crossing_dest`: within the rows of one device (1024 crossings), at most 64 crossings name the same destination, and in every draw some destination is named by exactly 64 of them.
All inputs are finite; a program needn't handle non-finite values.
Results may differ from the reference program's by a relative error of at most 0.0029.
Values may be sent and summed in bfloat16 or wider, within the bound.
A program may use at most 128 MiB of HBM per device.

```python
import math
import jax
import jax.numpy as jnp
import numpy as np
from jax import lax

L = 512
P_DEV = 1
K = 1024
GROUPS = 4
PARTICLES = 32
ZP = 64
YQ = 128
CAP = 64
N_SLAB = 8
N_GRP = 4


def place_ends(array, key, least, top_value):
    index_at = [jax.random.randint(jax.random.fold_in(key, axis), (), 0, length) for axis, length in enumerate(array.shape)]
    longest = array.shape.index(max(array.shape))
    next_to = index_at[:longest] + [(index_at[longest] + 1) % array.shape[longest]] + index_at[longest + 1:]
    return array.at[tuple(index_at)].set(least).at[tuple(next_to)].set(top_value)


def levels(own_key, shape, shards, low, high):
    loudness, own = 1.0, jax.random.fold_in(own_key, 6)
    for axis_at, blocks in shards:
        heights = jnp.exp(jax.random.uniform(jax.random.fold_in(own, axis_at), (blocks,), jnp.float32, low / len(shards), high / len(shards)))
        loudness = loudness * jnp.repeat(heights, shape[axis_at] // blocks).reshape([-1 if axis == axis_at else 1 for axis in range(len(shape))])
    return loudness


def routed_block(stream_key, own, number, rows, number_of, top, reach, skew):
    order = jax.random.permutation(stream_key, number_of)
    packed, ordinary = portions_of(number_of, rows * top, reach, skew, True), portions_of(number_of, rows * top, reach, skew, False)
    places = jnp.arange(number_of)

    def named(tallies, rotation):
        used = int((tallies > 0).sum())
        fixed = max(1, used // 4)
        moved = fixed + (places - fixed + rotation * (used - fixed)) % max(1, number_of - fixed)
        return jnp.zeros((number_of,), jnp.int32).at[order[jnp.where(places < fixed, places, moved)]].set(jnp.asarray(tallies, jnp.int32))

    tallies = jnp.where(number % 4 == 0, named(packed, number // 4), named(ordinary, number - number // 4 - 1))
    mixed = jax.random.permutation(jax.random.fold_in(own, 3), number_of)
    source_of, receiver = mixed[0:number_of // 2 * 2:2], mixed[1:number_of // 2 * 2:2]
    margin = jnp.minimum(tallies[source_of] - 1, reach - tallies[receiver]) // 2
    margin = jnp.where((source_of == order[0]) | (receiver == order[0]) | (tallies[receiver] == 0), 0, jnp.maximum(margin, 0))
    moved = jax.random.randint(jax.random.fold_in(own, 4), (number_of // 2,), 0, 1 << 20) % (margin + 1)
    tallies = tallies.at[source_of].add(-moved).at[receiver].add(moved)
    members = jnp.searchsorted(jnp.cumsum(tallies), jnp.arange(rows * top), side="right").astype(jnp.int32)
    table = members.reshape(top, rows).T
    table = table[jax.random.permutation(jax.random.fold_in(own, 1), rows)]
    rotation = jax.random.randint(jax.random.fold_in(own, 2), (rows, 1), 0, top)
    return jnp.take_along_axis(table, (jnp.arange(top)[None, :] + rotation) % top, axis=1)


def portions_of(number_of, total, reach, slope, full):
    weights = [(1 << 20) // math.isqrt(standing ** slope) + 1 for standing in range(1, number_of + 1)]
    largest = reach if full else min(reach, max(-(-total // number_of), total * weights[0] // sum(weights)))
    least = 1 if total - largest >= number_of - 1 else 0
    holding, spare = [largest] + [least] * (number_of - 1), total - largest - least * (number_of - 1)
    while spare > 0:
        movable = [i for i in range(1, number_of) if holding[i] < largest] or [i for i in range(1, number_of) if holding[i] < reach]
        mass, remaining = sum([weights[i] for i in movable]), spare
        for i in movable:
            addition = min(reach - holding[i], max(1, remaining * weights[i] // mass), spare)
            holding[i] = holding[i] + addition
            spare = spare - addition
    return np.array(holding)


def normal_values(own_key, dims, scale, most, split=(), kind=jnp.bfloat16):
    loudness = levels(own_key, dims, split, -0.22, 0.18) if split else 1.0
    drawn = jax.random.normal(own_key, dims, jnp.float32) * scale * loudness
    return jnp.minimum(jnp.maximum(drawn, -most), most).astype(kind)


def setup_inputs(seed: int = 0) -> dict:
    key_list = jax.random.split(jax.random.key(seed), 6)
    images = normal_values(key_list[0], (PARTICLES, L, L), 1.0, 6.0, ((0, 32),), jnp.float32)
    crossing_row = place_ends(jax.random.randint(key_list[1], (PARTICLES, K), 0, L), jax.random.fold_in(key_list[1], 1), 0, L - 1).astype(jnp.int32)
    crossing_dest_keys = jax.random.split(jax.random.fold_in(key_list[2], 1), PARTICLES * K // (P_DEV * K))
    crossing_dest_turns = jax.random.permutation(jax.random.fold_in(key_list[2], 3), PARTICLES * K // (P_DEV * K))
    crossing_dest = jax.vmap(lambda own, number: routed_block(jax.random.fold_in(key_list[2], 2), own, number, P_DEV * K, N_SLAB * N_GRP, 1, CAP, 2))(crossing_dest_keys, crossing_dest_turns).reshape((PARTICLES, K, 1))
    crossing_line = place_ends(jax.random.randint(key_list[3], (PARTICLES, K), 0, YQ), jax.random.fold_in(key_list[3], 1), 0, YQ - 1).astype(jnp.int32)
    interp_weight = jnp.clip(1.0 * jax.random.uniform(key_list[4], (PARTICLES, K, ZP), jnp.float32) ** levels(key_list[4], (PARTICLES, K, ZP), ((0, 32),), -0.2, 0.2), 0.0, 1.0).astype(jnp.bfloat16)
    return dict(images=images, crossing_row=crossing_row, crossing_dest=crossing_dest, crossing_line=crossing_line, interp_weight=interp_weight)


def reference(images, crossing_row, crossing_dest, crossing_line, interp_weight):
    plane_grid = jnp.arange(ZP, dtype=jnp.int32)

    def add_particle(volume, pieces):
        one_image, rows_of, dest_of, line_of, weight_of = pieces
        spectrum = jnp.fft.fft2(one_image, norm="ortho")
        picked = spectrum[rows_of]
        rows_low = jnp.concatenate([jnp.real(picked), jnp.imag(picked)], axis=1).astype(jnp.bfloat16)
        target = dest_of[:, 0]
        slab_of = target // GROUPS
        line_index = ((target % GROUPS) * YQ + line_of).astype(jnp.int32)
        plane_index = (slab_of[:, None] * ZP + plane_grid[None, :]).astype(jnp.int32)
        line_all = jnp.broadcast_to(line_index[:, None], plane_index.shape)
        spread_terms = weight_of.astype(jnp.float32)[:, :, None] * rows_low.astype(jnp.float32)[:, None, :]
        return volume.at[plane_index, line_all].add(spread_terms), None

    empty_volume = jnp.zeros((L, L, 2 * L), jnp.float32)
    volume, _ = lax.scan(add_particle, empty_volume, (images, crossing_row, crossing_dest, crossing_line, interp_weight))
    spectrum_field = lax.complex(volume[:, :, :L], volume[:, :, L:])
    spectrum_field = jnp.fft.ifft(spectrum_field, axis=2, norm="ortho")
    spectrum_field = jnp.fft.ifft(spectrum_field, axis=0, norm="ortho")
    stacked = jnp.stack([jnp.real(spectrum_field), jnp.imag(spectrum_field)])
    return jnp.transpose(stacked, (0, 3, 2, 1)).astype(jnp.float32)
```

```python
import functools
import math

import jax
import jax.numpy as jnp
import ml_dtypes
import numpy as np
from jax import lax
from jax.experimental import pallas as pl
from jax.experimental.pallas import tpu as pltpu
from jax.sharding import PartitionSpec as P

BLOCK_LINES = 8
CHUNK = 256
RADIX = 4
LANES = 128
BF16 = jnp.bfloat16
F32 = jnp.float32


def halves(table):
    high = table.astype(np.float32).astype(ml_dtypes.bfloat16)
    low = (table - high.astype(np.float64)).astype(ml_dtypes.bfloat16)
    return high, low


def forward_tables(length):
    index = np.arange(length)
    angle = 2.0 * math.pi / length * (index[:, None] * index[None, :] % length)
    return halves(np.stack([np.cos(angle), -np.sin(angle)]) / math.sqrt(length))


def inverse_tables(length):
    quarter = length // RADIX
    t, m, parts = np.arange(quarter), np.arange(quarter), []
    for q in range(RADIX):
        angle = 2.0 * math.pi / length * ((RADIX * t[:, None] + q) * m[None, :] % length)
        c, s = np.cos(angle), np.sin(angle)
        parts.append(np.block([[c, s], [-s, c]]))
    return halves(np.stack(parts) / math.sqrt(length))


def plane_order(planes):
    return np.arange(planes).reshape(planes // RADIX, RADIX).T.reshape(planes)


def repeat_table(length, planes):
    each = planes // RADIX
    row = np.arange(length)
    source = row // (length // RADIX) * each + row % each
    return (source[:, None] == np.arange(planes)[None, :]).astype(ml_dtypes.bfloat16)


def pick_kernel(planes, packed_ref, field_ref, out_ref, value_ref):
    packed = packed_ref[0].astype(F32)
    slots = packed.shape[0]
    rows = field_ref.shape[1]
    row = (packed[:, planes : planes + 1] * 256.0 + packed[:, planes + 1 : planes + 2]).astype(jnp.int32)
    hit = lax.broadcasted_iota(jnp.int32, (slots, rows), 1) == row
    picked = jnp.dot(hit.astype(F32).astype(BF16), field_ref[0], preferred_element_type=F32)
    width = picked.shape[1] // 2
    out_ref[...] = jnp.zeros((slots, LANES), F32)
    out_ref[:, :width] = picked[:, :width] + picked[:, width:]
    value_ref[...] = packed


def volume_kernel(planes, columns, sources, slots, offsets, stored, values, repeat, high, low, out, ordered, ordered_values, left, right, volume):
    block = pl.program_id(0)
    length = repeat.shape[0]
    quarter = length // RADIX
    pairs = 2 * columns
    each = planes // RADIX

    def move(p, position):
        begin = offsets[p, block]
        count = offsets[p, block + 1] - begin

        def step(k, carry):
            source, target = p * slots + begin + 8 * k, position + 8 * k
            ordered[pl.ds(target, 8), :] = stored[pl.ds(source, 8), :]
            ordered_values[pl.ds(target, 8), :] = values[pl.ds(source, 8), :]
            return carry

        lax.fori_loop(0, (count + 7) // 8, step, 0)
        return position + count

    total = lax.fori_loop(0, sources, move, 0)
    volume[...] = jnp.zeros_like(volume)
    slab_of_row = lax.broadcasted_iota(jnp.int32, (length, CHUNK), 0) % quarter // each
    line_of_row = lax.broadcasted_iota(jnp.int32, (BLOCK_LINES, CHUNK), 0) + block * BLOCK_LINES

    def add(chunk, carry):
        base = pl.multiple_of(chunk * CHUNK, CHUNK)
        present = lax.broadcasted_iota(jnp.int32, (1, CHUNK), 1) + base < total
        field = jnp.where(present, ordered[pl.ds(base, CHUNK), :].T, 0.0)[:pairs]
        turned = jnp.where(present, ordered_values[pl.ds(base, CHUNK), :].T, 0.0)
        weight = turned[:planes].astype(BF16)
        slab = turned[planes + 2 : planes + 3].astype(jnp.int32)
        line = turned[planes + 3 : planes + 4].astype(jnp.int32)
        spread = jnp.dot(repeat[...], weight, preferred_element_type=F32)
        spread = jnp.where(slab_of_row == slab, spread, 0.0).astype(BF16)
        right[:, :CHUNK] = spread
        right[:, CHUNK:] = spread
        mask = ((line_of_row == line) & present).astype(F32)
        field_high = field.astype(BF16).astype(F32)
        field_low = field - field_high
        left[:, :CHUNK] = (field_high[:, None, :] * mask[None]).reshape(pairs * BLOCK_LINES, CHUNK).astype(BF16)
        left[:, CHUNK:] = (field_low[:, None, :] * mask[None]).reshape(pairs * BLOCK_LINES, CHUNK).astype(BF16)
        volume[...] += lax.dot_general(
            left[...], right[...], (((1,), (1,)), ((), ())), preferred_element_type=F32
        )
        return carry

    lax.fori_loop(0, (total + CHUNK - 1) // CHUNK, add, 0)

    real, imag = [], []
    lines = columns * BLOCK_LINES
    for q in range(RADIX):
        at = slice(q * quarter, (q + 1) * quarter)
        part = jnp.concatenate([volume[:lines, at], volume[lines:, at]], axis=1)
        part_high = part.astype(BF16)
        part_low = (part - part_high.astype(F32)).astype(BF16)
        turned = jnp.dot(part_high, high[q], preferred_element_type=F32)
        turned += jnp.dot(part_low, high[q], preferred_element_type=F32)
        turned += jnp.dot(part_high, low[q], preferred_element_type=F32)
        real.append(turned[:, :quarter])
        imag.append(turned[:, quarter:])

    def put(r, re, im):
        at = slice(r * quarter, (r + 1) * quarter)
        out[0, :, :, at] = re.reshape(columns, BLOCK_LINES, quarter)
        out[1, :, :, at] = im.reshape(columns, BLOCK_LINES, quarter)

    even_re, even_im = real[0] + real[2], imag[0] + imag[2]
    odd_re, odd_im = real[1] + real[3], imag[1] + imag[3]
    put(0, even_re + odd_re, even_im + odd_im)
    put(2, even_re - odd_re, even_im - odd_im)
    even_re, even_im = real[0] - real[2], imag[0] - imag[2]
    odd_re, odd_im = real[1] - real[3], imag[1] - imag[3]
    put(1, even_re - odd_im, even_im + odd_re)
    put(3, even_re + odd_im, even_im - odd_re)


def local(images, crossing_row, crossing_dest, crossing_line, interp_weight):
    length = images.shape[1]
    crossings = crossing_row.shape[1]
    slab_count = lax.axis_size("slab")
    group_count = lax.axis_size("grp")
    devices_all = slab_count * group_count
    planes = length // slab_count
    columns = length // slab_count
    lines_per = length // group_count
    slots = min(crossings, slab_count * (2 * crossings // devices_all))
    blocks = lines_per // BLOCK_LINES

    turned = images[0].T.astype(BF16).reshape(slab_count, columns, length)
    turned = lax.all_to_all(turned, "slab", split_axis=0, concat_axis=0, tiled=True)
    turned = lax.all_gather(turned, "grp", axis=0)

    row, dest, line = crossing_row[0], crossing_dest[0, :, 0], crossing_line[0]
    group = dest % group_count
    key = (group * lines_per + line) * crossings + jnp.arange(crossings, dtype=jnp.int32)
    rank = jnp.sum((key[None, :] < key[:, None]).astype(jnp.int32), axis=1)
    before = jnp.sum((group[None, :] < group[:, None]).astype(jnp.int32), axis=1)
    slot = group * slots + rank - before
    meta = jnp.stack([row // 256, row % 256, dest // group_count, line, jnp.ones_like(line)], axis=1).astype(BF16)
    values = jnp.concatenate([interp_weight[0][:, plane_order(planes)], meta], axis=1)
    values = jnp.pad(values, ((0, 0), (0, LANES - values.shape[1])))
    place = (jnp.arange(group_count * slots, dtype=jnp.int32)[:, None] == slot[None, :]).astype(BF16)
    packed = jnp.dot(place, values, preferred_element_type=F32).astype(BF16)
    packed = packed.reshape(group_count, slots, LANES)
    packed = lax.all_to_all(packed, "grp", split_axis=0, concat_axis=0, tiled=True)
    packed = lax.all_gather(packed, "slab", axis=0).reshape(devices_all, slots, LANES)

    block_of = jnp.where(packed[:, :, planes + 4] > 0.5, packed[:, :, planes + 3].astype(jnp.int32) // BLOCK_LINES, blocks)
    offsets = jnp.sum(
        (block_of[:, None, :] < jnp.arange(blocks + 1, dtype=jnp.int32)[None, :, None]).astype(jnp.int32), axis=2
    )

    table_high, table_low = forward_tables(length)
    form = functools.partial(jnp.einsum, "rky,gsxy->gskrx", preferred_element_type=F32)
    field = form(table_high, turned) + form(table_low, turned)
    field_high = field.astype(BF16)
    field_low = (field - field_high.astype(F32)).astype(BF16)
    field = jnp.stack([field_high, field_low], axis=3).reshape(devices_all, length, 4 * columns)

    stored = pl.pallas_call(
        functools.partial(pick_kernel, planes),
        grid=(devices_all,),
        in_specs=[
            pl.BlockSpec((1, slots, LANES), lambda p: (p, 0, 0)),
            pl.BlockSpec(
                (1, length, 4 * columns), lambda p: (p % group_count * slab_count + p // group_count, 0, 0)
            ),
        ],
        out_specs=[pl.BlockSpec((slots, LANES), lambda p: (p, 0))] * 2,
        out_shape=[jax.ShapeDtypeStruct(((devices_all + 1) * slots, LANES), F32)] * 2,
        name="pick_rows",
    )(packed, field)

    small = devices_all * slots * 2 * LANES * 4 <= 20 * 2**20
    if not small:
        return whole_slice(stored, offsets, planes, columns, slots, blocks, length, lines_per, devices_all)
    return volume_call(stored, offsets, planes, columns, devices_all, slots, blocks, length, lines_per)


def volume_call(stored, offsets, planes, columns, sources, slots, blocks, length, lines_per):
    inverse_high, inverse_low = inverse_tables(length)
    vmem = pl.BlockSpec(memory_space=pltpu.VMEM)
    return pl.pallas_call(
        functools.partial(volume_kernel, planes, columns, sources, slots),
        grid_spec=pltpu.PrefetchScalarGridSpec(
            num_scalar_prefetch=1,
            grid=(blocks,),
            in_specs=[vmem] * 5,
            out_specs=pl.BlockSpec((2, columns, BLOCK_LINES, length), lambda b, _: (0, 0, b, 0)),
            scratch_shapes=[
                pltpu.VMEM((sources * slots + CHUNK, LANES), F32),
                pltpu.VMEM((sources * slots + CHUNK, LANES), F32),
                pltpu.VMEM((2 * columns * BLOCK_LINES, 2 * CHUNK), BF16),
                pltpu.VMEM((length, 2 * CHUNK), BF16),
                pltpu.VMEM((2 * columns * BLOCK_LINES, length), F32),
            ],
        ),
        out_shape=jax.ShapeDtypeStruct((2, columns, lines_per, length), F32),
        compiler_params=pltpu.CompilerParams(vmem_limit_bytes=58 * 2**20),
        name="volume",
    )(offsets, *stored, jnp.asarray(repeat_table(length, planes)), jnp.asarray(inverse_high), jnp.asarray(inverse_low))


def whole_slice(stored, offsets, planes, columns, slots, blocks, length, lines_per, sources):
    each = 32

    def add(part, running):
        some = [lax.dynamic_slice_in_dim(one, part * each * slots, (each + 1) * slots, axis=0) for one in stored]
        table = lax.dynamic_slice_in_dim(offsets, part * each, each, axis=0)
        return running + volume_call(some, table, planes, columns, each, slots, blocks, length, lines_per)

    return lax.fori_loop(0, sources // each, add, jnp.zeros((2, columns, lines_per, length), F32))


def solution(mesh):
    return jax.shard_map(
        local,
        mesh=mesh,
        in_specs=(
            P(("slab", "grp"), None, None),
            P(("slab", "grp"), None),
            P(("slab", "grp"), None, None),
            P(("slab", "grp"), None),
            P(("slab", "grp"), None, None),
        ),
        out_specs=P(None, "slab", "grp", None),
        check_vma=False,
    )
```
